32 devices in a mesh: group: 2 (over y), expert: 4 (over z), dp: 4 (over x, core).
Axes of the slice: x: 2, y: 2, z: 4, core: 2. Of those that a mesh axis runs over, the one named last changes fastest.
Arguments:
- output_gradient: bfloat16 [1024, 4096], P(('group', 'expert'), 'dp'), parts along dimension 0, may hold values from -6 to 6
- routes: int32 [1024, 8], P(('group', 'expert')), parts along dimension 0, may hold values from 0 to 15, all different within a row; in each aligned block of 128 rows (0 to 127, 128 to 255, ...) at most 96 rows name the same one
- routing_weight_values: float32 [1024, 8], P(('group', 'expert')), parts along dimension 0, may hold values from 0 to 1, as said below
- stored_hidden_input: bfloat16 [32, 384, 768], P(('group', 'expert'), None, 'dp'), parts along dimension 0, may hold values from -6 to 6
- weight: bfloat16 [16, 768, 4096], P('expert', None, 'dp'), may hold values from -0.125 to 0.125
- output_channel_scale: float32 [16, 4096], P('expert', 'dp'), may hold values from 0.5 to 2
- adapter_down_matrix: bfloat16 [16, 768, 64], P('expert', 'dp'), may hold values from -0.21875 to 0.21875
- adapter_up_matrix: bfloat16 [16, 64, 4096], P('expert', None, 'dp'), may hold values from -0.09375 to 0.09375
Outputs:
- intermediate_derivative: bfloat16 [32, 384, 768], P(('group', 'expert'), None, 'dp'), parts along dimension 0
- reducer_factor_derivative: float32 [32, 768, 64], P(('group', 'expert'), 'dp'), parts along dimension 0
- expander_factor_derivative: float32 [32, 64, 4096], P(('group', 'expert'), None, 'dp'), parts along dimension 0
- router_score_derivative: float32 [1024, 8], P(('group', 'expert')), parts along dimension 0
The draws below stay inside these ranges and needn't reach their ends.
There are 2 independent parts, one for each index of `group`. The reference program is written for one: setup_inputs(seed, part) draws one part's arguments, and reference() takes and returns one part's arrays. A program takes and returns all parts, laid end to end along the dimension named above; an argument that names none is the same for every part. Nothing has to cross between parts.
Inputs may be any that keep to these rules, and one draw needn't show every extreme that they name: `routes`: each token names 8 different experts. Among the tokens of one index of expert (aligned blocks of 128 tokens) no expert is named by more than 96 tokens, a bound that some block reaches. `routing_weight_values`: each row is positive and sums to one.
All inputs are finite; a program needn't handle non-finite values.
Results may differ from the reference program's by a relative error of at most 0.013.
Values may be sent and summed in bfloat16 or wider, within the bound.
A program may use at most 64 MiB of HBM per device.

```python
import math
import jax
import jax.numpy as jnp
import numpy as np
from jax import lax

MODEL_WIDTH = 4096
TOPK = 8
HALF_HIDDEN = 768
ADAPTER_RANK = 64
TOK = 128
EXPERT_TOTAL = 16
TOKENS = 512
CAP = 96
SLOTS = 384
N_EXPERT = 4
N_DP = 4


def draw_routing_weight_values(key, part):
    key = jax.random.fold_in(key, 11)
    spread = 0.5
    raw = jnp.exp(jax.random.uniform(key, (TOKENS, TOPK), jnp.float32, -spread, spread))
    return raw / jnp.sum(raw, axis=1, keepdims=True)


def with_spikes(entries, own_key, source, target, blocks, factor):
    owner, partner = [(jnp.arange(entries.shape[axis_at]) // (entries.shape[axis_at] // blocks)).reshape([-1 if axis == axis_at else 1 for axis in range(entries.ndim)]) for axis_at in (source, target)]
    chosen = jax.random.permutation(own_key, blocks)[partner]
    strong = (owner == chosen) | (owner == (partner + blocks // 2) % blocks)
    return jnp.where(strong, factor * entries, entries)


def block_scale(own_key, extent, split, low, top_value):
    def one(dim, shards_of):
        draws = jax.random.uniform(jax.random.fold_in(jax.random.fold_in(own_key, 6), dim), (shards_of,), jnp.float32, low / len(split), top_value / len(split))
        return jnp.repeat(jnp.exp(draws), extent[dim] // shards_of).reshape((-1,) + (1,) * (len(extent) - dim - 1))

    factor_of = one(*split[0])
    for cut in split[1:]:
        factor_of = factor_of * one(*cut)
    return factor_of


def deal_out(key, own, number, rows, count, top, limit, slope):
    ranking = jax.random.permutation(key, count)
    heavy_load, ordinary = shares(count, rows * top, limit, slope, True), shares(count, rows * top, limit, slope, False)
    places = jnp.arange(count)

    def named(tallies, rotation):
        used = int((tallies > 0).sum())
        fixed = max(1, used // 4)
        moved = fixed + (places - fixed + rotation * (used - fixed)) % max(1, count - fixed)
        return jnp.zeros((count,), jnp.int32).at[ranking[jnp.where(places < fixed, places, moved)]].set(jnp.asarray(tallies, jnp.int32))

    tallies = jnp.where(number % 4 == 0, named(heavy_load, number // 4), named(ordinary, number - number // 4 - 1))
    mixed = jax.random.permutation(jax.random.fold_in(own, 3), count)
    donor, receiver = mixed[0:count // 2 * 2:2], mixed[1:count // 2 * 2:2]
    slack = jnp.minimum(tallies[donor] - 1, limit - tallies[receiver]) // 2
    slack = jnp.where((donor == ranking[0]) | (receiver == ranking[0]) | (tallies[receiver] == 0), 0, jnp.maximum(slack, 0))
    moved = jax.random.randint(jax.random.fold_in(own, 4), (count // 2,), 0, 1 << 20) % (slack + 1)
    tallies = tallies.at[donor].add(-moved).at[receiver].add(moved)
    labels = jnp.searchsorted(jnp.cumsum(tallies), jnp.arange(rows * top), side="right").astype(jnp.int32)
    grid = labels.reshape(top, rows).T
    grid = grid[jax.random.permutation(jax.random.fold_in(own, 1), rows)]
    rotation = jax.random.randint(jax.random.fold_in(own, 2), (rows, 1), 0, top)
    return jnp.take_along_axis(grid, (jnp.arange(top)[None, :] + rotation) % top, axis=1)


def shares(amount, total, bound, slope, full):
    portions = [(1 << 20) // math.isqrt(rank ** slope) + 1 for rank in range(1, amount + 1)]
    largest = bound if full else min(bound, max(-(-total // amount), total * portions[0] // sum(portions)))
    least = 1 if total - largest >= amount - 1 else 0
    given, rest = [largest] + [least] * (amount - 1), total - largest - least * (amount - 1)
    while rest > 0:
        free = [i for i in range(1, amount) if given[i] < largest] or [i for i in range(1, amount) if given[i] < bound]
        mass, remaining = sum([portions[i] for i in free]), rest
        for i in free:
            more = min(bound - given[i], max(1, remaining * portions[i] // mass), rest)
            given[i] = given[i] + more
            rest = rest - more
    return np.array(given)


def normal_values(stream_key, extent, deviation, most, cuts=(), kind=jnp.bfloat16):
    array = deviation * jax.random.normal(stream_key, extent, jnp.float32)
    if cuts:
        array = array * block_scale(stream_key, extent, cuts, -0.22, 0.18)
    return jnp.clip(array, -most, most).astype(kind)


def heavy_noise(own_key, shape, deviation, limit, pieces, heavy, kind=jnp.bfloat16):
    values = deviation * jax.random.normal(own_key, shape, jnp.float32)
    if pieces:
        values = values * block_scale(own_key, shape, pieces, -0.22, 0.18)
    return jnp.clip(with_spikes(values, jax.random.fold_in(own_key, 3), *heavy), -limit, limit).astype(kind)


def setup_inputs(seed: int = 0, part: int = 0) -> dict:
    arg_keys = jax.random.split(jax.random.key(seed), 9)
    part_keys = jax.random.split(jax.random.fold_in(arg_keys[8], part), 9)
    output_gradient = normal_values(part_keys[0], (TOKENS, MODEL_WIDTH), 1.0, 6.0, ((0, 4), (1, 4)))
    routes_keys = jax.random.split(jax.random.fold_in(part_keys[1], 1), TOKENS // TOK)
    routes_turns = jax.random.permutation(jax.random.fold_in(part_keys[1], 3), TOKENS // TOK)
    routes = jax.vmap(lambda own, number: deal_out(jax.random.fold_in(part_keys[1], 2), own, number, TOK, EXPERT_TOTAL, TOPK, CAP, 2))(routes_keys, routes_turns).reshape((TOKENS, TOPK))
    routing_weight_values = draw_routing_weight_values(jax.random.fold_in(jax.random.fold_in(arg_keys[8], part), 71), part)
    stored_hidden_input = normal_values(part_keys[3], (EXPERT_TOTAL, SLOTS, HALF_HIDDEN), 1.0, 6.0, ((0, 4), (2, 4)))
    weight = heavy_noise(arg_keys[4], (EXPERT_TOTAL, HALF_HIDDEN, MODEL_WIDTH), MODEL_WIDTH ** -0.5, 0.125, ((0, 4), (2, 4)), (2, 1, 4, 2.0))
    output_channel_scale = jnp.clip(jnp.exp(math.log(2.0) - 1.3862944 * jax.random.uniform(arg_keys[5], (EXPERT_TOTAL, MODEL_WIDTH), jnp.float32) ** block_scale(arg_keys[5], (EXPERT_TOTAL, MODEL_WIDTH), ((0, 4), (1, 4)), -0.2, 0.2)), 0.5, 2.0)
    adapter_down_matrix = normal_values(arg_keys[6], (EXPERT_TOTAL, HALF_HIDDEN, ADAPTER_RANK), HALF_HIDDEN ** -0.5, 0.21875, ((0, 4), (1, 4)))
    adapter_up_matrix = normal_values(arg_keys[7], (EXPERT_TOTAL, ADAPTER_RANK, MODEL_WIDTH), MODEL_WIDTH ** -0.5, 0.09375, ((0, 4), (2, 4)))
    return dict(output_gradient=output_gradient, routes=routes, routing_weight_values=routing_weight_values, stored_hidden_input=stored_hidden_input, weight=weight, output_channel_scale=output_channel_scale, adapter_down_matrix=adapter_down_matrix, adapter_up_matrix=adapter_up_matrix)


correction_multiplier = 2.0


def reference(output_gradient, routes, routing_weight_values, stored_hidden_input, weight, output_channel_scale, adapter_down_matrix, adapter_up_matrix):
    gate_b = routing_weight_values.astype(jnp.bfloat16)
    blocks = routes.reshape(N_EXPERT, TOK * TOPK)
    onehot = (blocks[:, :, None] == jnp.arange(EXPERT_TOTAL, dtype=jnp.int32)[None, None, :]).astype(jnp.int32)
    ranks = jnp.sum(onehot * (jnp.cumsum(onehot, axis=1) - 1), axis=2)
    source = jnp.arange(N_EXPERT, dtype=jnp.int32)[:, None]
    target = (blocks * SLOTS + source * CAP + ranks).reshape(-1).astype(jnp.int32)
    pairs = TOKENS * TOPK
    slot_source = jnp.full((EXPERT_TOTAL * SLOTS,), pairs, jnp.int32).at[target].set(jnp.arange(pairs, dtype=jnp.int32))
    token_for_slot = (slot_source // TOPK).reshape(EXPERT_TOTAL, SLOTS)
    padded_rows = jnp.concatenate([output_gradient, jnp.zeros((1, MODEL_WIDTH), output_gradient.dtype)], axis=0)
    padded_gates = jnp.concatenate([gate_b.reshape(-1), jnp.zeros((1,), gate_b.dtype)])
    slot_gate_weights = padded_gates[slot_source].reshape(EXPERT_TOTAL, SLOTS)

    def single_expert_body(items):
        token_idx, gates_row, intermediate_features, w_mat, scale_row, down_adapter, b_mat = items
        incoming_derivative_lines = padded_rows[token_idx]
        scaled = (incoming_derivative_lines.astype(jnp.float32) * scale_row[None, :]).astype(jnp.bfloat16)
        parts = jnp.einsum('spd,fpd->psf', scaled.reshape(SLOTS, N_DP, MODEL_WIDTH // N_DP).astype(jnp.float32),
                           w_mat.reshape(HALF_HIDDEN, N_DP, MODEL_WIDTH // N_DP).astype(jnp.float32))
        rounded = lax.optimization_barrier(parts.astype(jnp.bfloat16))
        frozen_contribution = jnp.sum(rounded.astype(jnp.float32), axis=0)
        row_projection = jnp.dot(incoming_derivative_lines, b_mat.T, preferred_element_type=jnp.float32).astype(jnp.bfloat16)
        hidden_unit_gradient = frozen_contribution + correction_multiplier * jnp.dot(row_projection, down_adapter.T, preferred_element_type=jnp.float32)
        gate_col = gates_row.astype(jnp.float32)[:, None]
        intermediate_derivative = (gate_col * hidden_unit_gradient).astype(jnp.bfloat16)
        position_mixing_derivative = jnp.sum(intermediate_features.astype(jnp.float32) * hidden_unit_gradient, axis=1)
        hidden_proj = jnp.dot(intermediate_features, down_adapter, preferred_element_type=jnp.float32)
        mapped_weighted_product = (gate_col * row_projection.astype(jnp.float32)).astype(jnp.bfloat16)
        reducer_factor_derivative = correction_multiplier * jnp.dot(intermediate_features.T, mapped_weighted_product, preferred_element_type=jnp.float32)
        intermediate_weighted_product = (gate_col * hidden_proj).astype(jnp.bfloat16)
        expander_factor_derivative = correction_multiplier * jnp.dot(intermediate_weighted_product.T, incoming_derivative_lines, preferred_element_type=jnp.float32)
        return intermediate_derivative, reducer_factor_derivative, expander_factor_derivative, position_mixing_derivative

    intermediate_derivative, reducer_factor_derivative, expander_factor_derivative, position_mixing_derivative = lax.map(
        single_expert_body, (token_for_slot, slot_gate_weights, stored_hidden_input, weight, output_channel_scale, adapter_down_matrix, adapter_up_matrix))
    pair_dgate = position_mixing_derivative.reshape(-1)[target].reshape(TOKENS, TOPK)
    mean_term = jnp.sum(routing_weight_values * pair_dgate, axis=1, keepdims=True)
    router_score_derivative = routing_weight_values * (pair_dgate - mean_term)
    return intermediate_derivative, reducer_factor_derivative, expander_factor_derivative, router_score_derivative
```

```python
import jax
import jax.numpy as jnp
from jax import lax
from jax.sharding import PartitionSpec as P

correction_multiplier = 2.0


def local(
    output_gradient,
    routes,
    routing_weight_values,
    stored_hidden_input,
    weight,
    output_channel_scale,
    adapter_down_matrix,
    adapter_up_matrix,
):
    n_expert = lax.axis_size("expert")
    exp_dev = weight.shape[0]
    experts_all = exp_dev * n_expert
    slots = stored_hidden_input.shape[1]
    capacity = slots // n_expert
    tok_rows, top_count = routes.shape
    width_part = output_gradient.shape[1]
    bf16, f32 = jnp.bfloat16, jnp.float32

    packed = jnp.concatenate(
        [output_gradient, routes.astype(bf16), routing_weight_values.astype(bf16)], axis=1
    )
    everyone = lax.all_gather(packed, "expert", axis=0, tiled=True)
    rows_all = everyone[:, :width_part]
    routes_all = everyone[:, width_part : width_part + top_count].astype(f32).astype(jnp.int32)
    gates_all = everyone[:, width_part + top_count :].astype(f32)
    hidden_local = jnp.einsum(
        "mid,mda->mia", stored_hidden_input, adapter_down_matrix, preferred_element_type=f32
    )
    mine = lax.axis_index("expert") * exp_dev + jnp.arange(exp_dev, dtype=jnp.int32)
    hit = routes_all[None, :, :] == mine[:, None, None]
    named = jnp.any(hit, axis=2)
    token_gate = jnp.sum(jnp.where(hit, gates_all[None], 0.0), axis=2)
    before = (
        jnp.arange(tok_rows)[:, None] > jnp.arange(tok_rows)[None, :]
    ).astype(bf16)
    ranks = jnp.einsum(
        "ent,ut->enu",
        named.astype(bf16).reshape(exp_dev, n_expert, tok_rows),
        before,
        preferred_element_type=f32,
    ).astype(jnp.int32)
    slot = ranks + capacity * jnp.arange(n_expert, dtype=jnp.int32)[None, :, None]
    slot = jnp.where(named, slot.reshape(exp_dev, -1), -1)
    place = slot[:, None, :] == jnp.arange(slots, dtype=jnp.int32)[None, :, None]
    lines = jnp.einsum(
        "est,td->esd", place.astype(bf16), rows_all, preferred_element_type=f32
    ).astype(bf16)
    gate_col = jnp.sum(jnp.where(place, token_gate[:, None, :], 0.0), axis=2)[:, :, None]

    scaled = (lines.astype(f32) * output_channel_scale[:, None, :]).astype(bf16)
    row_local = jnp.einsum("awy,agy->awg", lines, adapter_up_matrix, preferred_element_type=f32)
    both = lax.psum(
        jnp.concatenate([row_local, hidden_local], axis=2).astype(bf16), "dp"
    )
    rank_count = adapter_up_matrix.shape[1]
    row_projection = both[:, :, :rank_count]
    hidden_proj = both[:, :, rank_count:].astype(f32)
    frozen_t = lax.psum_scatter(
        jnp.einsum("esd,efd->fes", scaled, weight, preferred_element_type=f32).astype(bf16),
        "dp",
        scatter_dimension=0,
        tiled=True,
    ).astype(f32)
    frozen_contribution = jnp.transpose(frozen_t, (1, 2, 0))
    hidden_unit_gradient = frozen_contribution + correction_multiplier * jnp.einsum(
        "jkh,jzh->jkz", row_projection, adapter_down_matrix, preferred_element_type=f32
    )
    intermediate_derivative = (gate_col * hidden_unit_gradient).astype(bf16)
    gate_part = jnp.sum(stored_hidden_input.astype(f32) * hidden_unit_gradient, axis=2)
    gated_proj = (gate_col * row_projection.astype(f32)).astype(bf16)
    reducer_factor_derivative = correction_multiplier * jnp.einsum(
        "esf,esr->efr", stored_hidden_input, gated_proj, preferred_element_type=f32
    )
    gated_hidden = (gate_col * hidden_proj).astype(bf16)
    expander_factor_derivative = correction_multiplier * jnp.einsum(
        "esr,esd->erd", gated_hidden, lines, preferred_element_type=f32
    )
    token_dgate = jnp.sum(jnp.where(place, gate_part[:, :, None], 0.0), axis=1)
    returned = lax.all_to_all(
        token_dgate.reshape(exp_dev, n_expert, tok_rows),
        "expert",
        split_axis=1,
        concat_axis=0,
        tiled=True,
    ).reshape(experts_all, tok_rows)
    summed = lax.psum(returned, "dp")
    named_by = routes.T[:, None, :] == jnp.arange(experts_all, dtype=jnp.int32)[None, :, None]
    pair_dgate = jnp.sum(jnp.where(named_by, summed[None], 0.0), axis=1).T
    mean_term = jnp.sum(routing_weight_values * pair_dgate, axis=1, keepdims=True)
    router_score_derivative = routing_weight_values * (pair_dgate - mean_term)
    return (
        intermediate_derivative,
        reducer_factor_derivative,
        expander_factor_derivative,
        router_score_derivative,
    )


def solution(mesh):
    return jax.shard_map(
        local,
        mesh=mesh,
        in_specs=(
            P(("group", "expert"), "dp"),
            P(("group", "expert"), None),
            P(("group", "expert"), None),
            P(("group", "expert"), None, "dp"),
            P("expert", None, "dp"),
            P("expert", "dp"),
            P("expert", "dp", None),
            P("expert", None, "dp"),
        ),
        out_specs=(
            P(("group", "expert"), None, "dp"),
            P(("group", "expert"), "dp", None),
            P(("group", "expert"), None, "dp"),
            P(("group", "expert"), None),
        ),
        check_vma=False,
    )
```

```python
import functools
import jax
import jax.numpy as jnp
from jax import lax
from jax.experimental import pallas as pl
from jax.experimental.pallas import tpu as pltpu
from jax.sharding import PartitionSpec as P

correction_multiplier = 2.0
bf16, f32 = jnp.bfloat16, jnp.float32


def dot(a, b, ca, cb):
    return lax.dot_general(a, b, (((ca,), (cb,)), ((), ())), preferred_element_type=f32)


def kernel(
    n_expert, n_dp,
    x_ref, routes_ref, gates_ref, h_ref, w_hbm, scale_ref, down_ref, up_ref,
    inter_ref, red_ref, exp_ref, out_ref,
    x_all, meta_send, meta_all, w_vmem, lines_ref, gcol_ref, dense_ref,
    hid, hid_sib, hid_chip, hid_x, row, row_sib, row_chip, row_x,
    fz, fz_sib, fz_chip, fz_x, dg_send, dg_recv, dg_part, dg_all,
    w_sem, ag_s, ag_r, mt_s, mt_r, hs_s, hs_r, hx_s, hx_r, rs_s, rs_r, rx_s, rx_r,
    fs_s, fs_r, fx_s, fx_r, ds_s, ds_r, dp_s, dp_r,
):
    exp_dev, hidden, width = w_vmem.shape
    slots = h_ref.shape[1]
    tok = x_ref.shape[0]
    capacity = slots // n_expert
    experts_all = exp_dev * n_expert
    top_count = routes_ref.shape[0]
    part = hidden // n_dp
    n_x = n_dp // 2
    me = lax.axis_index("expert")
    my_dp = lax.axis_index("dp")
    my_x, core = my_dp // 2, lax.rem(my_dp, 2)
    sibling = my_x * 2 + 1 - core
    blocked = capacity % 16 == 0

    for e in range(exp_dev):
        pltpu.make_async_copy(w_hbm.at[e], w_vmem.at[e], w_sem.at[e]).start()

    barrier = pltpu.get_barrier_semaphore()
    for d in range(1, n_expert):
        pl.semaphore_signal(barrier, inc=1, device_id={"expert": lax.rem(me + d, n_expert)})
    for d in range(1, n_dp):
        pl.semaphore_signal(barrier, inc=1, device_id={"dp": lax.rem(my_dp + d, n_dp)})

    ids = lax.broadcasted_iota(jnp.int32, (experts_all, tok), 0)
    named = jnp.zeros((experts_all, tok), f32)
    gate = jnp.zeros((experts_all, tok), f32)
    for k in range(top_count):
        eq = ids == routes_ref[k : k + 1, :]
        named = jnp.where(eq, 1.0, named)
        gate = jnp.where(eq, gates_ref[k : k + 1, :].astype(bf16).astype(f32), gate)
    earlier = (
        lax.broadcasted_iota(jnp.int32, (tok, tok), 0)
        < lax.broadcasted_iota(jnp.int32, (tok, tok), 1)
    )
    ranks = dot(named.astype(bf16), jnp.where(earlier, 1.0, 0.0).astype(bf16), 1, 0)
    ranks = jnp.where(named > 0.5, ranks, -1.0)
    for d in range(n_expert):
        meta_send[d, 0:exp_dev, :] = ranks[d * exp_dev : (d + 1) * exp_dev]
        meta_send[d, exp_dev : 2 * exp_dev, :] = gate[d * exp_dev : (d + 1) * exp_dev]

    pl.semaphore_wait(barrier, n_expert - 1 + n_dp - 1)

    def remote(src, dst, ss, rs, axis, peer):
        return pltpu.make_async_remote_copy(
            src_ref=src, dst_ref=dst, send_sem=ss, recv_sem=rs,
            device_id={axis: peer}, device_id_type=pl.DeviceIdType.MESH,
        )

    gathers = []
    for d in range(1, n_expert):
        to = lax.rem(me + d, n_expert)
        gathers.append(remote(meta_send.at[to], meta_all.at[me], mt_s.at[d], mt_r.at[d], "expert", to))
        gathers.append(remote(x_ref, x_all.at[me], ag_s.at[d], ag_r.at[d], "expert", to))
    for copy in gathers:
        copy.start()
    x_all[me] = x_ref[...]
    meta_all[me] = meta_send[me]

    for e in range(exp_dev):
        hid[e] = dot(down_ref[e], h_ref[e], 0, 1).astype(bf16)

    def pair(src, dst, ss, rs):
        return remote(src, dst, ss.at[0], rs.at[0], "dp", sibling)

    def across(src, dst, ss, rs):
        return [
            remote(src, dst.at[d], ss.at[d], rs.at[d], "dp", lax.rem(my_x + d, n_x) * 2 + core)
            for d in range(1, n_x)
        ]

    hid_pair = pair(hid, hid_sib, hs_s, hs_r)
    hid_pair.start()
    hid_pair.wait()
    hid_chip[...] = (hid[...].astype(f32) + hid_sib[...].astype(f32)).astype(bf16)
    hid_across = across(hid_chip, hid_x, hx_s, hx_r)
    for copy in hid_across:
        copy.start()
    for copy in gathers:
        copy.wait()

    def chosen(e, n):
        rows = capacity if blocked else slots
        place = lax.broadcasted_iota(jnp.int32, (rows, tok), 0).astype(f32)
        rank = meta_all[n, pl.ds(e, 1), :]
        if not blocked:
            rank = jnp.where(rank < 0.0, -1.0, rank + jnp.asarray(n * capacity, jnp.int32).astype(f32))
        return place == rank

    def gather_rows(e):
        if blocked:
            for n in range(n_expert):
                hit = chosen(e, n)
                lo = n * capacity
                lines_ref[e, lo : lo + capacity, :] = dot(
                    jnp.where(hit, 1.0, 0.0).astype(bf16), x_all[n], 1, 0
                ).astype(bf16)
                g = jnp.where(hit, meta_all[n, pl.ds(exp_dev + e, 1), :], 0.0)
                gcol_ref[e, lo : lo + capacity, :] = jnp.broadcast_to(
                    jnp.sum(g, axis=1, keepdims=True), (capacity, 128)
                )
        else:
            dense_ref[...] = jnp.zeros_like(dense_ref)
            gcol_ref[e] = jnp.zeros((slots, 128), f32)

            def step(n, carry):
                hit = chosen(e, n)
                dense_ref[...] += dot(jnp.where(hit, 1.0, 0.0).astype(bf16), x_all[n], 1, 0)
                g = jnp.where(hit, meta_all[n, pl.ds(exp_dev + e, 1), :], 0.0)
                gcol_ref[e] += jnp.broadcast_to(jnp.sum(g, axis=1, keepdims=True), (slots, 128))
                return carry

            lax.fori_loop(0, n_expert, step, 0)
            lines_ref[e] = dense_ref[...].astype(bf16)

    def fz_pair(e):
        return remote(fz.at[e, 1 - core], fz_sib.at[e], fs_s.at[e], fs_r.at[e], "dp", sibling)

    def fz_across(e):
        return [
            remote(
                fz_chip.at[e, d], fz_x.at[e, d], fx_s.at[e, d], fx_r.at[e, d],
                "dp", lax.rem(my_x + d, n_x) * 2 + core,
            )
            for d in range(1, n_x)
        ]

    def chip_sum(e, x):
        return fz[e, core, x].astype(f32) + fz_sib[e, x].astype(f32)

    def second(e):
        fz_pair(e).wait()
        for d in range(1, n_x):
            fz_chip[e, d] = chip_sum(e, lax.rem(my_x + d, n_x)).astype(bf16)
        for copy in fz_across(e):
            copy.start()

    def first(e, carry):
        gather_rows(e)
        lines = lines_ref[e]
        row[e] = dot(up_ref[e], lines, 1, 1).astype(bf16)
        scaled = (lines.astype(f32) * scale_ref[pl.ds(e, 1), :]).astype(bf16)
        pltpu.make_async_copy(w_hbm.at[e], w_vmem.at[e], w_sem.at[e]).wait()
        for q in range(n_dp):
            fz[e, q % 2, q // 2] = dot(
                w_vmem[e, q * part : (q + 1) * part, :], scaled, 1, 1
            ).astype(bf16)
        fz_pair(e).start()

        @pl.when(e > 0)
        def _():
            second(e - 1)

        return carry

    lax.fori_loop(0, exp_dev, first, 0)
    row_pair = pair(row, row_sib, rs_s, rs_r)
    row_pair.start()
    second(exp_dev - 1)
    row_pair.wait()
    row_chip[...] = (row[...].astype(f32) + row_sib[...].astype(f32)).astype(bf16)
    row_across = across(row_chip, row_x, rx_s, rx_r)
    for copy in row_across:
        copy.start()

    for copy in hid_across:
        copy.wait()

    def expander(e, carry):
        total = hid[e].astype(f32) + hid_sib[e].astype(f32)
        for d in range(1, n_x):
            total += hid_x[d, e].astype(f32)
        gate_row = jnp.transpose(gcol_ref[e])[0:1, :]
        exp_ref[e] = correction_multiplier * dot(
            (gate_row * total).astype(bf16), lines_ref[e], 1, 0
        )
        return carry

    lax.fori_loop(0, exp_dev, expander, 0)
    for copy in row_across:
        copy.wait()

    def last(e, carry):
        total = row[e].astype(f32) + row_sib[e].astype(f32)
        for d in range(1, n_x):
            total += row_x[d, e].astype(f32)
        row_proj = total.astype(bf16)
        gate_row = jnp.transpose(gcol_ref[e])[0:1, :]
        gated = (gate_row * row_proj.astype(f32)).astype(bf16)
        h = h_ref[e]
        red_ref[e] = correction_multiplier * dot(gated, h, 1, 0)
        for copy in fz_across(e):
            copy.wait()
        unit = chip_sum(e, my_x)
        for d in range(1, n_x):
            unit += fz_x[e, d].astype(f32)
        unit += correction_multiplier * dot(down_ref[e], row_proj, 1, 0)
        unit = jnp.transpose(unit)
        inter_ref[e] = (gcol_ref[e, :, 0:1] * unit).astype(bf16)
        dgate = jnp.sum(h.astype(f32) * unit, axis=1, keepdims=True)

        if blocked:
            for n in range(n_expert):
                lo = n * capacity
                dg_send[n, pl.ds(e, 1), :] = jnp.sum(
                    jnp.where(chosen(e, n), dgate[lo : lo + capacity], 0.0), axis=0, keepdims=True
                )
        else:
            def step(n, carry):
                dg_send[n, pl.ds(e, 1), :] = jnp.sum(
                    jnp.where(chosen(e, n), dgate, 0.0), axis=0, keepdims=True
                )
                return carry

            lax.fori_loop(0, n_expert, step, 0)
        return carry

    dg_send[...] = jnp.zeros_like(dg_send)
    lax.fori_loop(0, exp_dev, last, 0)

    back = []
    for d in range(1, n_expert):
        to = lax.rem(me + d, n_expert)
        back.append(remote(dg_send.at[to], dg_recv.at[me], ds_s.at[d], ds_r.at[d], "expert", to))
    for copy in back:
        copy.start()
    dg_recv[me] = dg_send[me]
    for copy in back:
        copy.wait()
    shares = [
        remote(dg_recv, dg_all.at[d], dp_s.at[d], dp_r.at[d], "dp", lax.rem(my_dp + d, n_dp))
        for d in range(1, n_dp)
    ]
    for copy in shares:
        copy.start()
    for copy in shares:
        copy.wait()
    order = [lax.rem(my_dp - p + n_dp, n_dp) for p in range(n_dp)]
    dg_all[0] = dg_recv[...]
    summed = dg_all[order[0]]
    for p in range(1, n_dp):
        summed += dg_all[order[p]]
    dg_part[...] = summed
    pair_dgate = jnp.zeros((top_count, tok), f32)
    for n in range(n_expert):
        for j in range(exp_dev):
            pair_dgate = jnp.where(
                routes_ref[...] == n * exp_dev + j, dg_part[n, j : j + 1, :], pair_dgate
            )
    weights = gates_ref[...]
    mean_term = jnp.sum(weights * pair_dgate, axis=0, keepdims=True)
    out_ref[...] = weights * (pair_dgate - mean_term)


def local(n_expert, n_dp, x, routes, gates, h, weight, scale, down, up):
    exp_dev, hidden, width = weight.shape
    slots = h.shape[1]
    tok, top_count = routes.shape
    rank = up.shape[1]
    part = hidden // n_dp
    n_x = n_dp // 2
    rows8 = -(-2 * exp_dev // 8) * 8
    blocked = (slots // n_expert) % 16 == 0
    vm = pltpu.VMEM
    dma = pltpu.SemaphoreType.DMA
    proj = (exp_dev, rank, slots)
    scratch = [
        vm((n_expert, tok, width), bf16), vm((n_expert, rows8, tok), f32),
        vm((n_expert, rows8, tok), f32), vm(weight.shape, bf16),
        vm((exp_dev, slots, width), bf16), vm((exp_dev, slots, 128), f32),
        vm((8, 128) if blocked else (slots, width), f32),
        vm(proj, bf16), vm(proj, bf16), vm(proj, bf16), vm((n_x,) + proj, bf16),
        vm(proj, bf16), vm(proj, bf16), vm(proj, bf16), vm((n_x,) + proj, bf16),
        vm((exp_dev, 2, n_x, part, slots), bf16), vm((exp_dev, n_x, part, slots), bf16),
        vm((exp_dev, n_x, part, slots), bf16), vm((exp_dev, n_x, part, slots), bf16),
        vm((n_expert, rows8, tok), f32), vm((n_expert, rows8, tok), f32),
        vm((n_expert, rows8, tok), f32), vm((n_dp, n_expert, rows8, tok), f32),
        dma((exp_dev,)),
        dma((n_expert,)), dma((n_expert,)), dma((n_expert,)), dma((n_expert,)),
        dma((1,)), dma((1,)), dma((n_x,)), dma((n_x,)),
        dma((1,)), dma((1,)), dma((n_x,)), dma((n_x,)),
        dma((exp_dev,)), dma((exp_dev,)), dma((exp_dev, n_x)), dma((exp_dev, n_x)),
        dma((n_expert,)), dma((n_expert,)), dma((n_dp,)), dma((n_dp,)),
    ]
    inside = pl.BlockSpec(memory_space=pltpu.VMEM)
    specs = [inside] * 8
    specs[4] = pl.BlockSpec(memory_space=pl.ANY)
    inter, red, expd, out = pl.pallas_call(
        functools.partial(kernel, n_expert, n_dp),
        out_shape=(
            jax.ShapeDtypeStruct(h.shape, bf16),
            jax.ShapeDtypeStruct((exp_dev, rank, part), f32),
            jax.ShapeDtypeStruct(up.shape, f32),
            jax.ShapeDtypeStruct((top_count, tok), f32),
        ),
        in_specs=specs,
        out_specs=(inside,) * 4,
        scratch_shapes=scratch,
        compiler_params=pltpu.CompilerParams(
            collective_id=0, has_side_effects=True, vmem_limit_bytes=52 * 2**20
        ),
    )(x, routes.T, gates.T, h, weight, scale, down, up)
    return inter, jnp.transpose(red, (0, 2, 1)), expd, out.T


def solution(mesh):
    return jax.shard_map(
        functools.partial(local, mesh.shape["expert"], mesh.shape["dp"]),
        mesh=mesh,
        in_specs=(
            P(("group", "expert"), "dp"),
            P(("group", "expert"), None),
            P(("group", "expert"), None),
            P(("group", "expert"), None, "dp"),
            P("expert", None, "dp"),
            P("expert", "dp"),
            P("expert", "dp", None),
            P("expert", None, "dp"),
        ),
        out_specs=(
            P(("group", "expert"), None, "dp"),
            P(("group", "expert"), "dp", None),
            P(("group", "expert"), None, "dp"),
            P(("group", "expert"), None),
        ),
        check_vma=False,
    )
```

```python
import functools
import jax
import jax.numpy as jnp
from jax import lax
from jax.experimental import pallas as pl
from jax.experimental.pallas import tpu as pltpu
from jax.sharding import PartitionSpec as P

correction_multiplier = 2.0
bf16, f32 = jnp.bfloat16, jnp.float32


def dot(a, b, ca, cb):
    return lax.dot_general(a, b, (((ca,), (cb,)), ((), ())), preferred_element_type=f32)


def kernel(
    n_expert, n_dp,
    x_ref, routes_hbm, gates_hbm, h_hbm, w_hbm, scale_hbm, down_hbm, up_hbm,
    inter_ref, red_ref, exp_ref, out_ref,
    routes_ref, gates_ref, h_ref, scale_ref, down_ref, up_ref, in_sem, own_sem,
    x_all, meta_send, meta_all, w_vmem, lines_ref, gcol_ref, dense_ref,
    hid, hid_sib, hid_chip, hid_x, row, row_sib, row_chip, row_x,
    fz, fz_sib, fz_chip, fz_x, dg_send, dg_recv, dg_part, dg_all,
    w_sem, right_s, right_r, left_s, left_r, mt_s, mt_r, hs_s, hs_r, hx_s, hx_r, rs_s, rs_r, rx_s, rx_r,
    fs_s, fs_r, fx_s, fx_r, ds_s, ds_r, dp_s, dp_r,
):
    exp_dev, hidden, width = w_vmem.shape
    slots = h_ref.shape[2]
    tok = x_ref.shape[0]
    capacity = slots // n_expert
    experts_all = exp_dev * n_expert
    top_count = routes_ref.shape[0]
    part = hidden // n_dp
    n_x = n_dp // 2
    me = lax.axis_index("expert")
    my_dp = lax.axis_index("dp")
    my_x, core = my_dp // 2, lax.rem(my_dp, 2)
    sibling = my_x * 2 + 1 - core
    blocked = capacity % 16 == 0

    loads = [
        pltpu.make_async_copy(src, dst, in_sem.at[i])
        for i, (src, dst) in enumerate(
            (
                (routes_hbm, routes_ref), (gates_hbm, gates_ref), (h_hbm, h_ref),
                (down_hbm, down_ref), (up_hbm, up_ref), (scale_hbm, scale_ref),
            )
        )
    ]
    for copy in loads:
        copy.start()
    own = pltpu.make_async_copy(x_ref, x_all.at[me], own_sem.at[0])
    own.start()
    for e in range(exp_dev):
        pltpu.make_async_copy(w_hbm.at[e], w_vmem.at[e], w_sem.at[e]).start()

    barrier = pltpu.get_barrier_semaphore()
    for d in range(1, n_expert):
        pl.semaphore_signal(barrier, inc=1, device_id={"expert": lax.rem(me + d, n_expert)})
    for d in range(1, n_dp):
        pl.semaphore_signal(barrier, inc=1, device_id={"dp": lax.rem(my_dp + d, n_dp)})

    loads[0].wait()
    loads[1].wait()
    ids = lax.broadcasted_iota(jnp.int32, (experts_all, tok), 0)
    named = jnp.zeros((experts_all, tok), f32)
    gate = jnp.zeros((experts_all, tok), f32)
    for k in range(top_count):
        eq = ids == routes_ref[k : k + 1, :]
        named = jnp.where(eq, 1.0, named)
        gate = jnp.where(eq, gates_ref[k : k + 1, :].astype(bf16).astype(f32), gate)
    earlier = (
        lax.broadcasted_iota(jnp.int32, (tok, tok), 0)
        < lax.broadcasted_iota(jnp.int32, (tok, tok), 1)
    )
    ranks = dot(named.astype(bf16), jnp.where(earlier, 1.0, 0.0).astype(bf16), 1, 0)
    ranks = jnp.where(named > 0.5, ranks, -1.0)
    for d in range(n_expert):
        meta_send[d, 0:exp_dev, :] = ranks[d * exp_dev : (d + 1) * exp_dev]
        meta_send[d, exp_dev : 2 * exp_dev, :] = gate[d * exp_dev : (d + 1) * exp_dev]

    pl.semaphore_wait(barrier, n_expert - 1 + n_dp - 1)

    def remote(src, dst, ss, rs, axis, peer):
        return pltpu.make_async_remote_copy(
            src_ref=src, dst_ref=dst, send_sem=ss, recv_sem=rs,
            device_id={axis: peer}, device_id_type=pl.DeviceIdType.MESH,
        )

    def hop(k, way):
        shard = me - way * (k - 1)
        ss, rs = (right_s, right_r) if way > 0 else (left_s, left_r)
        src = x_ref if k == 1 else x_all.at[shard]
        sends = (me + way >= 0) & (me + way < n_expert) & (shard >= 0) & (shard < n_expert)
        return sends, lambda: remote(
            src, x_all.at[shard], ss.at[k], rs.at[k], "expert", me + way
        )

    def arrival(k, way):
        shard = me - way * k
        rs = right_r if way > 0 else left_r
        ss = right_s if way > 0 else left_s
        comes = (shard >= 0) & (shard < n_expert)
        return shard, comes, lambda: remote(
            x_all.at[shard], x_all.at[shard], ss.at[k], rs.at[k], "expert", me - way
        )

    def send(k, way):
        sends, make = hop(k, way)

        @pl.when(sends)
        def _():
            make().start()

    gathers = []
    for d in range(1, n_expert):
        to = lax.rem(me + d, n_expert)
        gathers.append(remote(meta_send.at[to], meta_all.at[me], mt_s.at[d], mt_r.at[d], "expert", to))
    send(1, 1)
    send(1, -1)
    for copy in gathers:
        copy.start()
    meta_all[me] = meta_send[me]
    for copy in loads[2:]:
        copy.wait()

    for e in range(exp_dev):
        hid[e] = dot(down_ref[e], h_ref[e], 1, 0).astype(bf16)

    def pair(src, dst, ss, rs):
        return remote(src, dst, ss.at[0], rs.at[0], "dp", sibling)

    def across(src, dst, ss, rs):
        return [
            remote(src, dst.at[d], ss.at[d], rs.at[d], "dp", lax.rem(my_x + d, n_x) * 2 + core)
            for d in range(1, n_x)
        ]

    hid_pair = pair(hid, hid_sib, hs_s, hs_r)
    hid_pair.start()
    hid_pair.wait()
    hid_chip[...] = (hid[...].astype(f32) + hid_sib[...].astype(f32)).astype(bf16)
    hid_across = across(hid_chip, hid_x, hx_s, hx_r)
    for copy in hid_across:
        copy.start()
    for copy in gathers:
        copy.wait()
    own.wait()

    def chosen(e, n):
        rows = capacity if blocked else slots
        place = lax.broadcasted_iota(jnp.int32, (rows, tok), 0).astype(f32)
        rank = meta_all[n, pl.ds(e, 1), :]
        if not blocked:
            rank = jnp.where(rank < 0.0, -1.0, rank + jnp.asarray(n * capacity, jnp.int32).astype(f32))
        return place == rank

    def gather_block(n):
        def one(e, carry):
            hit = chosen(e, n)
            rows = pl.ds(pl.multiple_of(n * capacity, 16), capacity)
            lines_ref[e, rows, :] = dot(
                jnp.where(hit, 1.0, 0.0).astype(bf16), x_all[n], 1, 0
            ).astype(bf16)
            g = jnp.where(hit, meta_all[n, pl.ds(exp_dev + e, 1), :], 0.0)
            gcol_ref[e, rows, :] = jnp.broadcast_to(
                jnp.sum(g, axis=1, keepdims=True), (capacity, 128)
            )
            return carry

        lax.fori_loop(0, exp_dev, one, 0)

    if blocked:
        gather_block(me)
    for k in range(1, n_expert):
        came = []
        for way in (1, -1):
            shard, comes, make = arrival(k, way)

            @pl.when(comes)
            def _():
                make().wait_recv()

            if k + 1 < n_expert:
                send(k + 1, way)
            came.append((shard, comes))
        if blocked:
            for shard, comes in came:
                @pl.when(comes)
                def _():
                    gather_block(shard)

    def gather_rows(e):
        if not blocked:
            dense_ref[...] = jnp.zeros_like(dense_ref)
            gcol_ref[e] = jnp.zeros((slots, 128), f32)

            def step(n, carry):
                hit = chosen(e, n)
                dense_ref[...] += dot(jnp.where(hit, 1.0, 0.0).astype(bf16), x_all[n], 1, 0)
                g = jnp.where(hit, meta_all[n, pl.ds(exp_dev + e, 1), :], 0.0)
                gcol_ref[e] += jnp.broadcast_to(jnp.sum(g, axis=1, keepdims=True), (slots, 128))
                return carry

            lax.fori_loop(0, n_expert, step, 0)
            lines_ref[e] = dense_ref[...].astype(bf16)

    def fz_pair(e):
        return remote(fz.at[e, 1 - core], fz_sib.at[e], fs_s.at[e], fs_r.at[e], "dp", sibling)

    def fz_across(e):
        return [
            remote(
                fz_chip.at[e, d], fz_x.at[e, d], fx_s.at[e, d], fx_r.at[e, d],
                "dp", lax.rem(my_x + d, n_x) * 2 + core,
            )
            for d in range(1, n_x)
        ]

    def chip_sum(e, x):
        return fz[e, core, x].astype(f32) + fz_sib[e, x].astype(f32)

    def second(e):
        fz_pair(e).wait()
        for d in range(1, n_x):
            fz_chip[e, d] = chip_sum(e, lax.rem(my_x + d, n_x)).astype(bf16)
        for copy in fz_across(e):
            copy.start()

    def first(e, carry):
        gather_rows(e)
        lines = lines_ref[e]
        row[e] = dot(up_ref[e], lines, 1, 1).astype(bf16)
        scaled = (lines.astype(f32) * scale_ref[pl.ds(e, 1), :]).astype(bf16)
        pltpu.make_async_copy(w_hbm.at[e], w_vmem.at[e], w_sem.at[e]).wait()
        for q in range(n_dp):
            fz[e, q % 2, q // 2] = dot(
                w_vmem[e, q * part : (q + 1) * part, :], scaled, 1, 1
            ).astype(bf16)
        fz_pair(e).start()

        @pl.when(e > 0)
        def _():
            second(e - 1)

        return carry

    lax.fori_loop(0, exp_dev, first, 0)
    row_pair = pair(row, row_sib, rs_s, rs_r)
    row_pair.start()
    second(exp_dev - 1)
    row_pair.wait()
    row_chip[...] = (row[...].astype(f32) + row_sib[...].astype(f32)).astype(bf16)
    row_across = across(row_chip, row_x, rx_s, rx_r)
    for copy in row_across:
        copy.start()

    for copy in hid_across:
        copy.wait()

    def expander(e, carry):
        total = hid[e].astype(f32) + hid_sib[e].astype(f32)
        for d in range(1, n_x):
            total += hid_x[d, e].astype(f32)
        gate_row = jnp.transpose(gcol_ref[e])[0:1, :]
        exp_ref[e] = correction_multiplier * dot(
            (gate_row * total).astype(bf16), lines_ref[e], 1, 0
        )
        return carry

    lax.fori_loop(0, exp_dev, expander, 0)
    for copy in row_across:
        copy.wait()

    def last(e, carry):
        total = row[e].astype(f32) + row_sib[e].astype(f32)
        for d in range(1, n_x):
            total += row_x[d, e].astype(f32)
        row_proj = total.astype(bf16)
        gate_row = jnp.transpose(gcol_ref[e])[0:1, :]
        gated = (gate_row * row_proj.astype(f32)).astype(bf16)
        h = h_ref[e]
        red_ref[e] = correction_multiplier * dot(gated, h, 1, 1)
        for copy in fz_across(e):
            copy.wait()
        unit = chip_sum(e, my_x)
        for d in range(1, n_x):
            unit += fz_x[e, d].astype(f32)
        unit += correction_multiplier * dot(down_ref[e], row_proj, 0, 0)
        inter_ref[e] = (gate_row * unit).astype(bf16)
        dgate = jnp.sum(h.astype(f32) * unit, axis=0, keepdims=True)
        dgate = jnp.transpose(jnp.broadcast_to(dgate, (128, slots)))[:, 0:1]

        if blocked:
            for n in range(n_expert):
                lo = n * capacity
                dg_send[n, pl.ds(e, 1), :] = jnp.sum(
                    jnp.where(chosen(e, n), dgate[lo : lo + capacity], 0.0), axis=0, keepdims=True
                )
        else:
            def step(n, carry):
                dg_send[n, pl.ds(e, 1), :] = jnp.sum(
                    jnp.where(chosen(e, n), dgate, 0.0), axis=0, keepdims=True
                )
                return carry

            lax.fori_loop(0, n_expert, step, 0)
        return carry

    dg_send[...] = jnp.zeros_like(dg_send)
    lax.fori_loop(0, exp_dev, last, 0)

    for k in range(1, n_expert):
        for way in (1, -1):
            sends, make = hop(k, way)

            @pl.when(sends)
            def _():
                make().wait_send()

    back = []
    for d in range(1, n_expert):
        to = lax.rem(me + d, n_expert)
        back.append(remote(dg_send.at[to], dg_recv.at[me], ds_s.at[d], ds_r.at[d], "expert", to))
    for copy in back:
        copy.start()
    dg_recv[me] = dg_send[me]
    for copy in back:
        copy.wait()
    shares = [
        remote(dg_recv, dg_all.at[d], dp_s.at[d], dp_r.at[d], "dp", lax.rem(my_dp + d, n_dp))
        for d in range(1, n_dp)
    ]
    for copy in shares:
        copy.start()
    for copy in shares:
        copy.wait()
    order = [lax.rem(my_dp - p + n_dp, n_dp) for p in range(n_dp)]
    dg_all[0] = dg_recv[...]
    summed = dg_all[order[0]]
    for p in range(1, n_dp):
        summed += dg_all[order[p]]
    dg_part[...] = summed
    pair_dgate = jnp.zeros((top_count, tok), f32)
    for n in range(n_expert):
        for j in range(exp_dev):
            pair_dgate = jnp.where(
                routes_ref[...] == n * exp_dev + j, dg_part[n, j : j + 1, :], pair_dgate
            )
    weights = gates_ref[...]
    mean_term = jnp.sum(weights * pair_dgate, axis=0, keepdims=True)
    out_ref[...] = weights * (pair_dgate - mean_term)


def local(n_expert, n_dp, x, routes, gates, h, weight, scale, down, up):
    h, down = jnp.swapaxes(h, 1, 2), jnp.swapaxes(down, 1, 2)
    exp_dev, hidden, width = weight.shape
    slots = h.shape[2]
    tok, top_count = routes.shape
    rank = up.shape[1]
    part = hidden // n_dp
    n_x = n_dp // 2
    rows8 = -(-2 * exp_dev // 8) * 8
    blocked = (slots // n_expert) % 16 == 0
    vm = pltpu.VMEM
    dma = pltpu.SemaphoreType.DMA
    proj = (exp_dev, rank, slots)
    scratch = [
        vm(routes.shape[::-1], jnp.int32), vm(gates.shape[::-1], f32), vm(h.shape, bf16),
        vm(scale.shape, f32), vm(down.shape, bf16), vm(up.shape, bf16), dma((6,)), dma((1,)),
        vm((n_expert, tok, width), bf16), vm((n_expert, rows8, tok), f32),
        vm((n_expert, rows8, tok), f32), vm(weight.shape, bf16),
        vm((exp_dev, slots, width), bf16), vm((exp_dev, slots, 128), f32),
        vm((8, 128) if blocked else (slots, width), f32),
        vm(proj, bf16), vm(proj, bf16), vm(proj, bf16), vm((n_x,) + proj, bf16),
        vm(proj, bf16), vm(proj, bf16), vm(proj, bf16), vm((n_x,) + proj, bf16),
        vm((exp_dev, 2, n_x, part, slots), bf16), vm((exp_dev, n_x, part, slots), bf16),
        vm((exp_dev, n_x, part, slots), bf16), vm((exp_dev, n_x, part, slots), bf16),
        vm((n_expert, rows8, tok), f32), vm((n_expert, rows8, tok), f32),
        vm((n_expert, rows8, tok), f32), vm((n_dp, n_expert, rows8, tok), f32),
        dma((exp_dev,)),
        dma((n_expert,)), dma((n_expert,)), dma((n_expert,)), dma((n_expert,)),
        dma((n_expert,)), dma((n_expert,)), dma((1,)), dma((1,)), dma((n_x,)), dma((n_x,)),
        dma((1,)), dma((1,)), dma((n_x,)), dma((n_x,)),
        dma((exp_dev,)), dma((exp_dev,)), dma((exp_dev, n_x)), dma((exp_dev, n_x)),
        dma((n_expert,)), dma((n_expert,)), dma((n_dp,)), dma((n_dp,)),
    ]
    inside = pl.BlockSpec(memory_space=pltpu.VMEM)
    specs = [pl.BlockSpec(memory_space=pltpu.HBM)] * 8
    inter, red, expd, out = pl.pallas_call(
        functools.partial(kernel, n_expert, n_dp),
        out_shape=(
            jax.ShapeDtypeStruct(h.shape, bf16),
            jax.ShapeDtypeStruct((exp_dev, rank, part), f32),
            jax.ShapeDtypeStruct(up.shape, f32),
            jax.ShapeDtypeStruct((top_count, tok), f32),
        ),
        in_specs=specs,
        out_specs=(inside,) * 4,
        scratch_shapes=scratch,
        compiler_params=pltpu.CompilerParams(
            collective_id=0, has_side_effects=True, vmem_limit_bytes=52 * 2**20
        ),
    )(x, routes.T, gates.T, h, weight, scale, down, up)
    return jnp.swapaxes(inter, 1, 2), jnp.transpose(red, (0, 2, 1)), expd, out.T


def solution(mesh):
    return jax.shard_map(
        functools.partial(local, mesh.shape["expert"], mesh.shape["dp"]),
        mesh=mesh,
        in_specs=(
            P(("group", "expert"), "dp"),
            P(("group", "expert"), None),
            P(("group", "expert"), None),
            P(("group", "expert"), None, "dp"),
            P("expert", None, "dp"),
            P("expert", "dp"),
            P("expert", "dp", None),
            P("expert", None, "dp"),
        ),
        out_specs=(
            P(("group", "expert"), None, "dp"),
            P(("group", "expert"), "dp", None),
            P(("group", "expert"), None, "dp"),
            P(("group", "expert"), None),
        ),
        check_vma=False,
    )
```

```python
import functools
import jax
import jax.numpy as jnp
from jax import lax
from jax.experimental import pallas as pl
from jax.experimental.pallas import tpu as pltpu
from jax.sharding import PartitionSpec as P

correction_multiplier = 2.0
bf16, f32 = jnp.bfloat16, jnp.float32


def dot(a, b, ca, cb):
    return lax.dot_general(a, b, (((ca,), (cb,)), ((), ())), preferred_element_type=f32)


def kernel(
    n_expert, n_dp,
    x_ref, routes_hbm, gates_hbm, h_hbm, w_hbm, scale_hbm, down_hbm, up_hbm,
    inter_ref, red_ref, exp_ref, out_ref,
    routes_ref, gates_ref, h_ref, scale_ref, down_ref, up_ref, in_sem, own_sem,
    x_all, meta_send, meta_all, w_vmem, lines_ref, gcol_ref, dense_ref,
    hid, hid_sib, hid_chip, hid_x, row, row_sib, row_chip, row_x,
    fz, fz_sib, fz_chip, fz_x, dg_send, dg_recv, dg_part, dg_all,
    w_sem, right_s, right_r, left_s, left_r, mt_s, mt_r, hs_s, hs_r, hx_s, hx_r, rs_s, rs_r, rx_s, rx_r,
    fs_s, fs_r, fx_s, fx_r, ds_s, ds_r, dp_s, dp_r,
):
    exp_dev, hidden, width = w_vmem.shape
    slots = h_ref.shape[2]
    tok = x_ref.shape[0]
    capacity = slots // n_expert
    experts_all = exp_dev * n_expert
    top_count = routes_ref.shape[0]
    part = hidden // n_dp
    n_x = n_dp // 2
    me = lax.axis_index("expert")
    my_dp = lax.axis_index("dp")
    my_x, core = my_dp // 2, lax.rem(my_dp, 2)
    sibling = my_x * 2 + 1 - core
    blocked = capacity % 16 == 0

    loads = [
        pltpu.make_async_copy(src, dst, in_sem.at[i])
        for i, (src, dst) in enumerate(
            (
                (routes_hbm, routes_ref), (gates_hbm, gates_ref), (h_hbm, h_ref),
                (down_hbm, down_ref), (up_hbm, up_ref), (scale_hbm, scale_ref),
            )
        )
    ]
    for copy in loads:
        copy.start()
    own = pltpu.make_async_copy(x_ref, x_all.at[me], own_sem.at[0])
    own.start()
    for e in range(exp_dev):
        pltpu.make_async_copy(w_hbm.at[e], w_vmem.at[e], w_sem.at[e]).start()

    barrier = pltpu.get_barrier_semaphore()
    for d in range(1, n_expert):
        pl.semaphore_signal(barrier, inc=1, device_id={"expert": lax.rem(me + d, n_expert)})
    for d in range(1, n_dp):
        pl.semaphore_signal(barrier, inc=1, device_id={"dp": lax.rem(my_dp + d, n_dp)})

    loads[0].wait()
    loads[1].wait()
    ids = lax.broadcasted_iota(jnp.int32, (experts_all, tok), 0)
    named = jnp.zeros((experts_all, tok), f32)
    gate = jnp.zeros((experts_all, tok), f32)
    for k in range(top_count):
        eq = ids == routes_ref[k : k + 1, :]
        named = jnp.where(eq, 1.0, named)
        gate = jnp.where(eq, gates_ref[k : k + 1, :].astype(bf16).astype(f32), gate)
    earlier = (
        lax.broadcasted_iota(jnp.int32, (tok, tok), 0)
        < lax.broadcasted_iota(jnp.int32, (tok, tok), 1)
    )
    ranks = dot(named.astype(bf16), jnp.where(earlier, 1.0, 0.0).astype(bf16), 1, 0)
    ranks = jnp.where(named > 0.5, ranks, -1.0)
    for d in range(n_expert):
        meta_send[d, 0:exp_dev, :] = ranks[d * exp_dev : (d + 1) * exp_dev]
        meta_send[d, exp_dev : 2 * exp_dev, :] = gate[d * exp_dev : (d + 1) * exp_dev]

    pl.semaphore_wait(barrier, n_expert - 1 + n_dp - 1)

    def remote(src, dst, ss, rs, axis, peer):
        return pltpu.make_async_remote_copy(
            src_ref=src, dst_ref=dst, send_sem=ss, recv_sem=rs,
            device_id={axis: peer}, device_id_type=pl.DeviceIdType.MESH,
        )

    def hop(k, way):
        shard = me - way * (k - 1)
        ss, rs = (right_s, right_r) if way > 0 else (left_s, left_r)
        src = x_ref if k == 1 else x_all.at[shard]
        sends = (me + way >= 0) & (me + way < n_expert) & (shard >= 0) & (shard < n_expert)
        return sends, lambda: remote(
            src, x_all.at[shard], ss.at[k], rs.at[k], "expert", me + way
        )

    def arrival(k, way):
        shard = me - way * k
        rs = right_r if way > 0 else left_r
        ss = right_s if way > 0 else left_s
        comes = (shard >= 0) & (shard < n_expert)
        return shard, comes, lambda: remote(
            x_all.at[shard], x_all.at[shard], ss.at[k], rs.at[k], "expert", me - way
        )

    def send(k, way):
        sends, make = hop(k, way)

        @pl.when(sends)
        def _():
            make().start()

    gathers = []
    for d in range(1, n_expert):
        to = lax.rem(me + d, n_expert)
        gathers.append(remote(meta_send.at[to], meta_all.at[me], mt_s.at[d], mt_r.at[d], "expert", to))
    send(1, 1)
    send(1, -1)
    for copy in gathers:
        copy.start()
    meta_all[me] = meta_send[me]
    for copy in loads[2:]:
        copy.wait()

    for e in range(exp_dev):
        hid[e] = dot(down_ref[e], h_ref[e], 1, 0).astype(bf16)

    def pair(src, dst, ss, rs):
        return remote(src, dst, ss.at[0], rs.at[0], "dp", sibling)

    def across(src, dst, ss, rs):
        return [
            remote(src, dst.at[d], ss.at[d], rs.at[d], "dp", lax.rem(my_x + d, n_x) * 2 + core)
            for d in range(1, n_x)
        ]

    hid_pair = pair(hid, hid_sib, hs_s, hs_r)
    hid_pair.start()
    hid_pair.wait()
    hid_chip[...] = (hid[...].astype(f32) + hid_sib[...].astype(f32)).astype(bf16)
    hid_across = across(hid_chip, hid_x, hx_s, hx_r)
    for copy in hid_across:
        copy.start()
    for copy in gathers:
        copy.wait()
    own.wait()

    def chosen(e, n):
        rows = capacity if blocked else slots
        place = lax.broadcasted_iota(jnp.int32, (rows, tok), 0).astype(f32)
        rank = meta_all[n, pl.ds(e, 1), :]
        if not blocked:
            rank = jnp.where(rank < 0.0, -1.0, rank + jnp.asarray(n * capacity, jnp.int32).astype(f32))
        return place == rank

    def gather_block(n):
        def one(e, carry):
            hit = chosen(e, n)
            rows = pl.ds(pl.multiple_of(n * capacity, 16), capacity)
            lines_ref[e, rows, :] = dot(
                jnp.where(hit, 1.0, 0.0).astype(bf16), x_all[n], 1, 0
            ).astype(bf16)
            g = jnp.where(hit, meta_all[n, pl.ds(exp_dev + e, 1), :], 0.0)
            gcol_ref[e, rows, :] = jnp.broadcast_to(
                jnp.sum(g, axis=1, keepdims=True), (capacity, 128)
            )
            return carry

        lax.fori_loop(0, exp_dev, one, 0)

    if blocked:
        gather_block(me)
    for k in range(1, n_expert):
        came = []
        for way in (1, -1):
            shard, comes, make = arrival(k, way)

            @pl.when(comes)
            def _():
                make().wait_recv()

            if k + 1 < n_expert:
                send(k + 1, way)
            came.append((shard, comes))
        if blocked:
            for shard, comes in came:
                @pl.when(comes)
                def _():
                    gather_block(shard)

    def gather_rows(e):
        if not blocked:
            dense_ref[...] = jnp.zeros_like(dense_ref)
            gcol_ref[e] = jnp.zeros((slots, 128), f32)

            def step(n, carry):
                hit = chosen(e, n)
                dense_ref[...] += dot(jnp.where(hit, 1.0, 0.0).astype(bf16), x_all[n], 1, 0)
                g = jnp.where(hit, meta_all[n, pl.ds(exp_dev + e, 1), :], 0.0)
                gcol_ref[e] += jnp.broadcast_to(jnp.sum(g, axis=1, keepdims=True), (slots, 128))
                return carry

            lax.fori_loop(0, n_expert, step, 0)
            lines_ref[e] = dense_ref[...].astype(bf16)

    def fz_pair(e):
        return remote(fz.at[e, 1 - core], fz_sib.at[e], fs_s.at[e], fs_r.at[e], "dp", sibling)

    def fz_across(e):
        return [
            remote(
                fz_chip.at[e, d], fz_x.at[e, d], fx_s.at[e, d], fx_r.at[e, d],
                "dp", lax.rem(my_x + d, n_x) * 2 + core,
            )
            for d in range(1, n_x)
        ]

    def chip_sum(e, x):
        return fz[e, core, x].astype(f32) + fz_sib[e, x].astype(f32)

    def second(e):
        fz_pair(e).wait()
        for d in range(1, n_x):
            fz_chip[e, d] = chip_sum(e, lax.rem(my_x + d, n_x)).astype(bf16)
        for copy in fz_across(e):
            copy.start()

    def first(e, carry):
        gather_rows(e)
        lines = lines_ref[e]
        row[e] = dot(up_ref[e], lines, 1, 1).astype(bf16)
        scaled = (lines.astype(f32) * scale_ref[pl.ds(e, 1), :]).astype(bf16)
        pltpu.make_async_copy(w_hbm.at[e], w_vmem.at[e], w_sem.at[e]).wait()
        for q in range(n_dp):
            fz[e, q % 2, q // 2] = dot(
                w_vmem[e, q * part : (q + 1) * part, :], scaled, 1, 1
            ).astype(bf16)
        fz_pair(e).start()

        @pl.when(e > 0)
        def _():
            second(e - 1)

        return carry

    lax.fori_loop(0, exp_dev, first, 0)
    row_pair = pair(row, row_sib, rs_s, rs_r)
    row_pair.start()
    second(exp_dev - 1)
    row_pair.wait()
    row_chip[...] = (row[...].astype(f32) + row_sib[...].astype(f32)).astype(bf16)
    row_across = across(row_chip, row_x, rx_s, rx_r)
    for copy in row_across:
        copy.start()

    for copy in hid_across:
        copy.wait()

    def expander(e, carry):
        total = hid[e].astype(f32) + hid_sib[e].astype(f32)
        for d in range(1, n_x):
            total += hid_x[d, e].astype(f32)
        gate_row = jnp.transpose(gcol_ref[e])[0:1, :]
        exp_ref[e] = correction_multiplier * dot(
            (gate_row * total).astype(bf16), lines_ref[e], 1, 0
        )
        return carry

    lax.fori_loop(0, exp_dev, expander, 0)
    for copy in row_across:
        copy.wait()

    def last(e, carry):
        total = row[e].astype(f32) + row_sib[e].astype(f32)
        for d in range(1, n_x):
            total += row_x[d, e].astype(f32)
        row_proj = total.astype(bf16)
        gate_row = jnp.transpose(gcol_ref[e])[0:1, :]
        gated = (gate_row * row_proj.astype(f32)).astype(bf16)
        h = h_ref[e]
        red_ref[e] = correction_multiplier * dot(gated, h, 1, 1)
        for copy in fz_across(e):
            copy.wait()
        unit = chip_sum(e, my_x)
        for d in range(1, n_x):
            unit += fz_x[e, d].astype(f32)
        unit += correction_multiplier * dot(down_ref[e], row_proj, 0, 0)
        inter_ref[e] = (gate_row * unit).astype(bf16)
        dgate = jnp.sum(h.astype(f32) * unit, axis=0, keepdims=True)
        dgate = jnp.transpose(jnp.broadcast_to(dgate, (128, slots)))[:, 0:1]

        if blocked:
            for n in range(n_expert):
                lo = n * capacity
                dg_send[n, pl.ds(e, 1), :] = jnp.sum(
                    jnp.where(chosen(e, n), dgate[lo : lo + capacity], 0.0), axis=0, keepdims=True
                )
        else:
            def step(n, carry):
                dg_send[n, pl.ds(e, 1), :] = jnp.sum(
                    jnp.where(chosen(e, n), dgate, 0.0), axis=0, keepdims=True
                )
                return carry

            lax.fori_loop(0, n_expert, step, 0)
        return carry

    dg_send[...] = jnp.zeros_like(dg_send)
    lax.fori_loop(0, exp_dev, last, 0)

    for k in range(1, n_expert):
        for way in (1, -1):
            sends, make = hop(k, way)

            @pl.when(sends)
            def _():
                make().wait_send()

    back = []
    for d in range(1, n_expert):
        to = lax.rem(me + d, n_expert)
        back.append(remote(dg_send.at[to], dg_recv.at[me], ds_s.at[d], ds_r.at[d], "expert", to))
    for copy in back:
        copy.start()
    dg_recv[me] = dg_send[me]
    for copy in back:
        copy.wait()
    shares = [
        remote(dg_recv, dg_all.at[d], dp_s.at[d], dp_r.at[d], "dp", lax.rem(my_dp + d, n_dp))
        for d in range(1, n_dp)
    ]
    for copy in shares:
        copy.start()
    for copy in shares:
        copy.wait()
    order = [lax.rem(my_dp - p + n_dp, n_dp) for p in range(n_dp)]
    dg_all[0] = dg_recv[...]
    summed = dg_all[order[0]]
    for p in range(1, n_dp):
        summed += dg_all[order[p]]
    dg_part[...] = summed
    pair_dgate = jnp.zeros((top_count, tok), f32)
    for n in range(n_expert):
        for j in range(exp_dev):
            pair_dgate = jnp.where(
                routes_ref[...] == n * exp_dev + j, dg_part[n, j : j + 1, :], pair_dgate
            )
    weights = gates_ref[...]
    mean_term = jnp.sum(weights * pair_dgate, axis=0, keepdims=True)
    out_ref[...] = weights * (pair_dgate - mean_term)


def local(n_expert, n_dp, x, routes, gates, h, weight, scale, down, up):
    h, down = jnp.swapaxes(h, 1, 2), jnp.swapaxes(down, 1, 2)
    exp_dev, hidden, width = weight.shape
    slots = h.shape[2]
    tok, top_count = routes.shape
    rank = up.shape[1]
    part = hidden // n_dp
    n_x = n_dp // 2
    rows8 = -(-2 * exp_dev // 8) * 8
    blocked = (slots // n_expert) % 16 == 0
    vm = pltpu.VMEM
    dma = pltpu.SemaphoreType.DMA
    proj = (exp_dev, rank, slots)
    scratch = [
        vm(routes.shape[::-1], jnp.int32), vm(gates.shape[::-1], f32), vm(h.shape, bf16),
        vm(scale.shape, f32), vm(down.shape, bf16), vm(up.shape, bf16), dma((6,)), dma((1,)),
        vm((n_expert, tok, width), bf16), vm((n_expert, rows8, tok), f32),
        vm((n_expert, rows8, tok), f32), vm(weight.shape, bf16),
        vm((exp_dev, slots, width), bf16), vm((exp_dev, slots, 128), f32),
        vm((8, 128) if blocked else (slots, width), f32),
        vm(proj, bf16), vm(proj, bf16), vm(proj, bf16), vm((n_x,) + proj, bf16),
        vm(proj, bf16), vm(proj, bf16), vm(proj, bf16), vm((n_x,) + proj, bf16),
        vm((exp_dev, 2, n_x, part, slots), bf16), vm((exp_dev, n_x, part, slots), bf16),
        vm((exp_dev, n_x, part, slots), bf16), vm((exp_dev, n_x, part, slots), bf16),
        vm((n_expert, rows8, tok), f32), vm((n_expert, rows8, tok), f32),
        vm((n_expert, rows8, tok), f32), vm((n_dp, n_expert, rows8, tok), f32),
        dma((exp_dev,)),
        dma((n_expert,)), dma((n_expert,)), dma((n_expert,)), dma((n_expert,)),
        dma((n_expert,)), dma((n_expert,)), dma((1,)), dma((1,)), dma((n_x,)), dma((n_x,)),
        dma((1,)), dma((1,)), dma((n_x,)), dma((n_x,)),
        dma((exp_dev,)), dma((exp_dev,)), dma((exp_dev, n_x)), dma((exp_dev, n_x)),
        dma((n_expert,)), dma((n_expert,)), dma((n_dp,)), dma((n_dp,)),
    ]
    inside = pl.BlockSpec(memory_space=pltpu.VMEM)
    specs = [pl.BlockSpec(memory_space=pltpu.HBM)] * 8
    inter, red, expd, out = pl.pallas_call(
        functools.partial(kernel, n_expert, n_dp),
        out_shape=(
            jax.ShapeDtypeStruct(h.shape, bf16),
            jax.ShapeDtypeStruct((exp_dev, rank, part), f32),
            jax.ShapeDtypeStruct(up.shape, f32),
            jax.ShapeDtypeStruct((top_count, tok), f32),
        ),
        in_specs=specs,
        out_specs=(inside,) * 4,
        scratch_shapes=scratch,
        compiler_params=pltpu.CompilerParams(
            collective_id=0, has_side_effects=True, vmem_limit_bytes=63 * 2**20
        ),
    )(x, routes.T, gates.T, h, weight, scale, down, up)
    return jnp.swapaxes(inter, 1, 2), jnp.transpose(red, (0, 2, 1)), expd, out.T


def solution(mesh):
    return jax.shard_map(
        functools.partial(local, mesh.shape["expert"], mesh.shape["dp"]),
        mesh=mesh,
        in_specs=(
            P(("group", "expert"), "dp"),
            P(("group", "expert"), None),
            P(("group", "expert"), None),
            P(("group", "expert"), None, "dp"),
            P("expert", None, "dp"),
            P("expert", "dp"),
            P("expert", "dp", None),
            P("expert", None, "dp"),
        ),
        out_specs=(
            P(("group", "expert"), None, "dp"),
            P(("group", "expert"), "dp", None),
            P(("group", "expert"), None, "dp"),
            P(("group", "expert"), None),
        ),
        check_vma=False,
    )
```

```python
import functools
import jax
import jax.numpy as jnp
from jax import lax
from jax.experimental import pallas as pl
from jax.experimental.pallas import tpu as pltpu
from jax.sharding import PartitionSpec as P

correction_multiplier = 2.0
bf16, f32 = jnp.bfloat16, jnp.float32


def dot(a, b, ca, cb):
    return lax.dot_general(a, b, (((ca,), (cb,)), ((), ())), preferred_element_type=f32)


def kernel(
    n_expert, n_dp,
    x_ref, routes_hbm, gates_hbm, h_hbm, w_hbm, scale_hbm, down_hbm, up_hbm,
    inter_ref, red_ref, exp_ref, out_ref,
    routes_ref, gates_ref, h_ref, scale_ref, down_ref, up_ref, in_sem, own_sem, unit_ref,
    x_all, meta_send, meta_all, w_vmem, lines_ref, gcol_ref, dense_ref,
    hid, hid_sib, hid_chip, hid_x, row, row_sib, row_chip, row_x,
    fz, fz_sib, fz_chip, fz_x, dg_send, dg_recv, dg_part, dg_all,
    w_sem, right_s, right_r, left_s, left_r, mt_s, mt_r, hs_s, hs_r, hx_s, hx_r, rs_s, rs_r, rx_s, rx_r,
    fs_s, fs_r, fx_s, fx_r, ds_s, ds_r, dp_s, dp_r,
):
    exp_dev, hidden, width = w_vmem.shape
    slots = h_ref.shape[2]
    tok = x_ref.shape[0]
    capacity = slots // n_expert
    experts_all = exp_dev * n_expert
    top_count = routes_ref.shape[0]
    part = hidden // n_dp
    n_x = n_dp // 2
    me = lax.axis_index("expert")
    my_dp = lax.axis_index("dp")
    my_x, core = my_dp // 2, lax.rem(my_dp, 2)
    sibling = my_x * 2 + 1 - core
    blocked = capacity % 16 == 0

    loads = [
        pltpu.make_async_copy(src, dst, in_sem.at[i])
        for i, (src, dst) in enumerate(
            (
                (routes_hbm, routes_ref), (gates_hbm, gates_ref), (h_hbm, h_ref),
                (down_hbm, down_ref), (up_hbm, up_ref), (scale_hbm, scale_ref),
            )
        )
    ]
    for copy in loads:
        copy.start()
    own = pltpu.make_async_copy(x_ref, x_all.at[me], own_sem.at[0])
    own.start()
    for e in range(exp_dev):
        pltpu.make_async_copy(w_hbm.at[e], w_vmem.at[e], w_sem.at[e]).start()

    barrier = pltpu.get_barrier_semaphore()
    for d in range(1, n_expert):
        pl.semaphore_signal(barrier, inc=1, device_id={"expert": lax.rem(me + d, n_expert)})
    for d in range(1, n_dp):
        pl.semaphore_signal(barrier, inc=1, device_id={"dp": lax.rem(my_dp + d, n_dp)})

    loads[0].wait()
    loads[1].wait()
    ids = lax.broadcasted_iota(jnp.int32, (experts_all, tok), 0)
    named = jnp.zeros((experts_all, tok), f32)
    gate = jnp.zeros((experts_all, tok), f32)
    for k in range(top_count):
        eq = ids == routes_ref[k : k + 1, :]
        named = jnp.where(eq, 1.0, named)
        gate = jnp.where(eq, gates_ref[k : k + 1, :].astype(bf16).astype(f32), gate)
    earlier = (
        lax.broadcasted_iota(jnp.int32, (tok, tok), 0)
        < lax.broadcasted_iota(jnp.int32, (tok, tok), 1)
    )
    ranks = dot(named.astype(bf16), jnp.where(earlier, 1.0, 0.0).astype(bf16), 1, 0)
    ranks = jnp.where(named > 0.5, ranks, -1.0)
    for d in range(n_expert):
        meta_send[d, 0:exp_dev, :] = ranks[d * exp_dev : (d + 1) * exp_dev]
        meta_send[d, exp_dev : 2 * exp_dev, :] = gate[d * exp_dev : (d + 1) * exp_dev]

    pl.semaphore_wait(barrier, n_expert - 1 + n_dp - 1)

    def remote(src, dst, ss, rs, axis, peer):
        return pltpu.make_async_remote_copy(
            src_ref=src, dst_ref=dst, send_sem=ss, recv_sem=rs,
            device_id={axis: peer}, device_id_type=pl.DeviceIdType.MESH,
        )

    def hop(k, way):
        shard = me - way * (k - 1)
        ss, rs = (right_s, right_r) if way > 0 else (left_s, left_r)
        src = x_ref if k == 1 else x_all.at[shard]
        sends = (me + way >= 0) & (me + way < n_expert) & (shard >= 0) & (shard < n_expert)
        return sends, lambda: remote(
            src, x_all.at[shard], ss.at[k], rs.at[k], "expert", me + way
        )

    def arrival(k, way):
        shard = me - way * k
        rs = right_r if way > 0 else left_r
        ss = right_s if way > 0 else left_s
        comes = (shard >= 0) & (shard < n_expert)
        return shard, comes, lambda: remote(
            x_all.at[shard], x_all.at[shard], ss.at[k], rs.at[k], "expert", me - way
        )

    def send(k, way):
        sends, make = hop(k, way)

        @pl.when(sends)
        def _():
            make().start()

    gathers = []
    for d in range(1, n_expert):
        to = lax.rem(me + d, n_expert)
        gathers.append(remote(meta_send.at[to], meta_all.at[me], mt_s.at[d], mt_r.at[d], "expert", to))
    send(1, 1)
    send(1, -1)
    for copy in gathers:
        copy.start()
    meta_all[me] = meta_send[me]
    for copy in loads[2:]:
        copy.wait()

    for e in range(exp_dev):
        hid[e] = dot(down_ref[e], h_ref[e], 1, 0).astype(bf16)

    def pair(src, dst, ss, rs):
        return remote(src, dst, ss.at[0], rs.at[0], "dp", sibling)

    def across(src, dst, ss, rs):
        return [
            remote(src, dst.at[d], ss.at[d], rs.at[d], "dp", lax.rem(my_x + d, n_x) * 2 + core)
            for d in range(1, n_x)
        ]

    hid_pair = pair(hid, hid_sib, hs_s, hs_r)
    hid_pair.start()
    hid_pair.wait()
    hid_chip[...] = (hid[...].astype(f32) + hid_sib[...].astype(f32)).astype(bf16)
    hid_across = across(hid_chip, hid_x, hx_s, hx_r)
    for copy in hid_across:
        copy.start()
    for copy in gathers:
        copy.wait()
    own.wait()

    def chosen(e, n):
        rows = capacity if blocked else slots
        place = lax.broadcasted_iota(jnp.int32, (rows, tok), 0).astype(f32)
        rank = meta_all[n, pl.ds(e, 1), :]
        if not blocked:
            rank = jnp.where(rank < 0.0, -1.0, rank + jnp.asarray(n * capacity, jnp.int32).astype(f32))
        return place == rank

    def fz_pair(e):
        return remote(fz.at[e, 1 - core], fz_sib.at[e], fs_s.at[e], fs_r.at[e], "dp", sibling)

    def fz_across(e):
        return [
            remote(
                fz_chip.at[e, d], fz_x.at[e, d], fx_s.at[e, d], fx_r.at[e, d],
                "dp", lax.rem(my_x + d, n_x) * 2 + core,
            )
            for d in range(1, n_x)
        ]

    def chip_sum(e, x):
        return fz[e, core, x].astype(f32) + fz_sib[e, x].astype(f32)

    def second(e):
        fz_pair(e).wait()
        for d in range(1, n_x):
            fz_chip[e, d] = chip_sum(e, lax.rem(my_x + d, n_x)).astype(bf16)
        for copy in fz_across(e):
            copy.start()

    def gather_block(n):
        rows = pl.ds(pl.multiple_of(n * capacity, 16), capacity)
        for e in range(exp_dev):
            hit = chosen(e, n)
            lines = dot(jnp.where(hit, 1.0, 0.0).astype(bf16), x_all[n], 1, 0)
            lines_ref[e, rows, :] = lines.astype(bf16)
            g = jnp.where(hit, meta_all[n, pl.ds(exp_dev + e, 1), :], 0.0)
            gcol_ref[e, rows, :] = jnp.broadcast_to(
                jnp.sum(g, axis=1, keepdims=True), (capacity, 128)
            )
            scaled = (lines * scale_ref[e : e + 1, :]).astype(bf16)
            for q in range(n_dp):
                fz[n, q % 2, q // 2, :, e * capacity : (e + 1) * capacity] = dot(
                    w_vmem[e, q * part : (q + 1) * part, :], scaled, 1, 1
                ).astype(bf16)
        fz_pair(n).start()

    if blocked:
        for e in range(exp_dev):
            pltpu.make_async_copy(w_hbm.at[e], w_vmem.at[e], w_sem.at[e]).wait()
        gather_block(me)
        second(me)
    for k in range(1, n_expert):
        came = []
        for way in (1, -1):
            shard, comes, make = arrival(k, way)

            @pl.when(comes)
            def _():
                make().wait_recv()

            if k + 1 < n_expert:
                send(k + 1, way)
            came.append((shard, comes))
        if blocked:
            for act in (gather_block, second):
                for shard, comes in came:
                    @pl.when(comes)
                    def _():
                        act(shard)

    def gather_rows(e):
        if not blocked:
            dense_ref[...] = jnp.zeros_like(dense_ref)
            gcol_ref[e] = jnp.zeros((slots, 128), f32)

            def step(n, carry):
                hit = chosen(e, n)
                dense_ref[...] += dot(jnp.where(hit, 1.0, 0.0).astype(bf16), x_all[n], 1, 0)
                g = jnp.where(hit, meta_all[n, pl.ds(exp_dev + e, 1), :], 0.0)
                gcol_ref[e] += jnp.broadcast_to(jnp.sum(g, axis=1, keepdims=True), (slots, 128))
                return carry

            lax.fori_loop(0, n_expert, step, 0)
            lines_ref[e] = dense_ref[...].astype(bf16)

    def first(e, carry):
        gather_rows(e)
        lines = lines_ref[e]
        row[e] = dot(up_ref[e], lines, 1, 1).astype(bf16)
        if blocked:
            return carry
        scaled = (lines.astype(f32) * scale_ref[pl.ds(e, 1), :]).astype(bf16)
        pltpu.make_async_copy(w_hbm.at[e], w_vmem.at[e], w_sem.at[e]).wait()
        for q in range(n_dp):
            fz[e, q % 2, q // 2] = dot(
                w_vmem[e, q * part : (q + 1) * part, :], scaled, 1, 1
            ).astype(bf16)
        fz_pair(e).start()

        @pl.when(e > 0)
        def _():
            second(e - 1)

        return carry

    lax.fori_loop(0, exp_dev, first, 0)
    row_pair = pair(row, row_sib, rs_s, rs_r)
    row_pair.start()
    if not blocked:
        second(exp_dev - 1)
    row_pair.wait()
    row_chip[...] = (row[...].astype(f32) + row_sib[...].astype(f32)).astype(bf16)
    row_across = across(row_chip, row_x, rx_s, rx_r)
    for copy in row_across:
        copy.start()

    for copy in hid_across:
        copy.wait()

    def expander(e, carry):
        total = hid[e].astype(f32) + hid_sib[e].astype(f32)
        for d in range(1, n_x):
            total += hid_x[d, e].astype(f32)
        gate_row = jnp.transpose(gcol_ref[e])[0:1, :]
        exp_ref[e] = correction_multiplier * dot(
            (gate_row * total).astype(bf16), lines_ref[e], 1, 0
        )
        return carry

    lax.fori_loop(0, exp_dev, expander, 0)
    for copy in row_across:
        copy.wait()

    def last(e, carry):
        total = row[e].astype(f32) + row_sib[e].astype(f32)
        for d in range(1, n_x):
            total += row_x[d, e].astype(f32)
        row_proj = total.astype(bf16)
        gate_row = jnp.transpose(gcol_ref[e])[0:1, :]
        gated = (gate_row * row_proj.astype(f32)).astype(bf16)
        h = h_ref[e]
        red_ref[e] = correction_multiplier * dot(gated, h, 1, 1)
        unit = unit_ref[e] + correction_multiplier * dot(down_ref[e], row_proj, 0, 0)
        inter_ref[e] = (gate_row * unit).astype(bf16)
        dgate = jnp.sum(h.astype(f32) * unit, axis=0, keepdims=True)
        dgate = jnp.transpose(jnp.broadcast_to(dgate, (128, slots)))[:, 0:1]

        if blocked:
            for n in range(n_expert):
                lo = n * capacity
                dg_send[n, pl.ds(e, 1), :] = jnp.sum(
                    jnp.where(chosen(e, n), dgate[lo : lo + capacity], 0.0), axis=0, keepdims=True
                )
        else:
            def step(n, carry):
                dg_send[n, pl.ds(e, 1), :] = jnp.sum(
                    jnp.where(chosen(e, n), dgate, 0.0), axis=0, keepdims=True
                )
                return carry

            lax.fori_loop(0, n_expert, step, 0)
        return carry

    for c in range(n_expert if blocked else exp_dev):
        for copy in fz_across(c):
            copy.wait()
        total = chip_sum(c, my_x)
        for d in range(1, n_x):
            total += fz_x[c, d].astype(f32)
        if blocked:
            for e in range(exp_dev):
                unit_ref[e, :, c * capacity : (c + 1) * capacity] = total[
                    :, e * capacity : (e + 1) * capacity
                ]
        else:
            unit_ref[c] = total

    dg_send[...] = jnp.zeros_like(dg_send)
    lax.fori_loop(0, exp_dev, last, 0)

    for k in range(1, n_expert):
        for way in (1, -1):
            sends, make = hop(k, way)

            @pl.when(sends)
            def _():
                make().wait_send()

    back = []
    for d in range(1, n_expert):
        to = lax.rem(me + d, n_expert)
        back.append(remote(dg_send.at[to], dg_recv.at[me], ds_s.at[d], ds_r.at[d], "expert", to))
    for copy in back:
        copy.start()
    dg_recv[me] = dg_send[me]
    for copy in back:
        copy.wait()
    shares = [
        remote(dg_recv, dg_all.at[d], dp_s.at[d], dp_r.at[d], "dp", lax.rem(my_dp + d, n_dp))
        for d in range(1, n_dp)
    ]
    for copy in shares:
        copy.start()
    for copy in shares:
        copy.wait()
    order = [lax.rem(my_dp - p + n_dp, n_dp) for p in range(n_dp)]
    dg_all[0] = dg_recv[...]
    summed = dg_all[order[0]]
    for p in range(1, n_dp):
        summed += dg_all[order[p]]
    dg_part[...] = summed
    pair_dgate = jnp.zeros((top_count, tok), f32)
    for n in range(n_expert):
        for j in range(exp_dev):
            pair_dgate = jnp.where(
                routes_ref[...] == n * exp_dev + j, dg_part[n, j : j + 1, :], pair_dgate
            )
    weights = gates_ref[...]
    mean_term = jnp.sum(weights * pair_dgate, axis=0, keepdims=True)
    out_ref[...] = weights * (pair_dgate - mean_term)


def local(n_expert, n_dp, x, routes, gates, h, weight, scale, down, up):
    h, down = jnp.swapaxes(h, 1, 2), jnp.swapaxes(down, 1, 2)
    exp_dev, hidden, width = weight.shape
    slots = h.shape[2]
    tok, top_count = routes.shape
    rank = up.shape[1]
    part = hidden // n_dp
    n_x = n_dp // 2
    rows8 = -(-2 * exp_dev // 8) * 8
    blocked = (slots // n_expert) % 16 == 0
    chunks = n_expert if blocked else exp_dev
    lanes = exp_dev * (slots // n_expert) if blocked else slots
    vm = pltpu.VMEM
    dma = pltpu.SemaphoreType.DMA
    proj = (exp_dev, rank, slots)
    scratch = [
        vm(routes.shape[::-1], jnp.int32), vm(gates.shape[::-1], f32), vm(h.shape, bf16),
        vm(scale.shape, f32), vm(down.shape, bf16), vm(up.shape, bf16), dma((6,)), dma((1,)), vm((exp_dev, part, slots), f32),
        vm((n_expert, tok, width), bf16), vm((n_expert, rows8, tok), f32),
        vm((n_expert, rows8, tok), f32), vm(weight.shape, bf16),
        vm((exp_dev, slots, width), bf16), vm((exp_dev, slots, 128), f32),
        vm((8, 128) if blocked else (slots, width), f32),
        vm(proj, bf16), vm(proj, bf16), vm(proj, bf16), vm((n_x,) + proj, bf16),
        vm(proj, bf16), vm(proj, bf16), vm(proj, bf16), vm((n_x,) + proj, bf16),
        vm((chunks, 2, n_x, part, lanes), bf16), vm((chunks, n_x, part, lanes), bf16),
        vm((chunks, n_x, part, lanes), bf16), vm((chunks, n_x, part, lanes), bf16),
        vm((n_expert, rows8, tok), f32), vm((n_expert, rows8, tok), f32),
        vm((n_expert, rows8, tok), f32), vm((n_dp, n_expert, rows8, tok), f32),
        dma((exp_dev,)),
        dma((n_expert,)), dma((n_expert,)), dma((n_expert,)), dma((n_expert,)),
        dma((n_expert,)), dma((n_expert,)), dma((1,)), dma((1,)), dma((n_x,)), dma((n_x,)),
        dma((1,)), dma((1,)), dma((n_x,)), dma((n_x,)),
        dma((chunks,)), dma((chunks,)), dma((chunks, n_x)), dma((chunks, n_x)),
        dma((n_expert,)), dma((n_expert,)), dma((n_dp,)), dma((n_dp,)),
    ]
    inside = pl.BlockSpec(memory_space=pltpu.VMEM)
    specs = [pl.BlockSpec(memory_space=pltpu.HBM)] * 8
    inter, red, expd, out = pl.pallas_call(
        functools.partial(kernel, n_expert, n_dp),
        out_shape=(
            jax.ShapeDtypeStruct(h.shape, bf16),
            jax.ShapeDtypeStruct((exp_dev, rank, part), f32),
            jax.ShapeDtypeStruct(up.shape, f32),
            jax.ShapeDtypeStruct((top_count, tok), f32),
        ),
        in_specs=specs,
        out_specs=(inside,) * 4,
        scratch_shapes=scratch,
        compiler_params=pltpu.CompilerParams(
            collective_id=0, has_side_effects=True, vmem_limit_bytes=63 * 2**20
        ),
    )(x, routes.T, gates.T, h, weight, scale, down, up)
    return jnp.swapaxes(inter, 1, 2), jnp.transpose(red, (0, 2, 1)), expd, out.T


def solution(mesh):
    return jax.shard_map(
        functools.partial(local, mesh.shape["expert"], mesh.shape["dp"]),
        mesh=mesh,
        in_specs=(
            P(("group", "expert"), "dp"),
            P(("group", "expert"), None),
            P(("group", "expert"), None),
            P(("group", "expert"), None, "dp"),
            P("expert", None, "dp"),
            P("expert", "dp"),
            P("expert", "dp", None),
            P("expert", None, "dp"),
        ),
        out_specs=(
            P(("group", "expert"), None, "dp"),
            P(("group", "expert"), "dp", None),
            P(("group", "expert"), None, "dp"),
            P(("group", "expert"), None),
        ),
        check_vma=False,
    )
```
